32 devices in a mesh: gx: 4 (over y, core), gy: 2 (over x), gz: 4 (over z).
Axes of the slice: x: 2, y: 2, z: 4, core: 2. Of those that a mesh axis runs over, the one named last changes fastest.
Arguments:
- source_field: float32 [2, 64, 32, 512], P(None, 'gx', 'gy', 'gz'), may hold values from -6 to 6
- mach_number: bfloat16 [64, 32, 512], P('gx', 'gy', 'gz'), may hold values from 0.14941406 to 0.59765625
Outputs:
- correction: float32 [2, 64, 32, 512], P(None, 'gx', 'gy', 'gz')
The draws below stay inside these ranges and needn't reach their ends.
All inputs are finite; a program needn't handle non-finite values.
Results may differ from the reference program's by a relative error of at most 0.0003.
Values sent between devices are 32-bit elements; how exact they have to be, the bound alone decides.
A program may use at most 128 MiB of HBM per device.

```python
import math
import jax
import jax.numpy as jnp

LEVELS = 5
PRE = 2
POST = 2
COARSE_SWEEPS = 6
NX = 64
NY = 32
NZ = 512


def draw_source_field(key, part):
    extent = (2, NX, NY, NZ)
    result = jnp.clip(jax.random.normal(key, extent, jnp.float32), -6.0, 6.0)
    return result.astype(jnp.float32)


def shard_levels(stream_key, dims, shards, least, largest):
    def one(dim, parts):
        heights = jax.random.uniform(jax.random.fold_in(jax.random.fold_in(stream_key, 6), dim), (parts,), jnp.float32, least / len(shards), largest / len(shards))
        return jnp.repeat(jnp.exp(heights), dims[dim] // parts).reshape((-1,) + (1,) * (len(dims) - dim - 1))

    factor_of = one(*shards[0])
    for cut in shards[1:]:
        factor_of = factor_of * one(*cut)
    return factor_of


def setup_inputs(seed: int = 0) -> dict:
    streams_of = jax.random.split(jax.random.key(seed), 3)
    return {
        "source_field": draw_source_field(jax.random.fold_in(streams_of[2], 71), 0),
        "mach_number": jnp.clip(jnp.exp(math.log(0.59765625) - 1.3862944 * jax.random.uniform(streams_of[1], (NX, NY, NZ), jnp.float32) ** shard_levels(streams_of[1], (NX, NY, NZ), ((0, 4), (1, 2), (2, 4)), -0.2, 0.2)), 0.14941406, 0.59765625).astype(jnp.bfloat16),
    }


wave_step = 0.25
jacobi_weight = 0.5


def complex_times(values, factor):
    real_part = values[0] * factor[0] - values[1] * factor[1]
    imaginary = values[0] * factor[1] + values[1] * factor[0]
    return jnp.stack([real_part, imaginary])


def inverse_diagonal(mach_field, grid_level):
    diffusion_scale = 0.25 ** grid_level
    wave_square = wave_step * wave_step
    axial_weight = 1.0 - mach_field * mach_field
    diagonal_real = diffusion_scale * (2.0 * axial_weight + 4.0) - wave_square
    diagonal_imaginary = 0.5 * wave_square
    modulus = diagonal_real * diagonal_real + diagonal_imaginary * diagonal_imaginary
    return jnp.stack([diagonal_real / modulus, -diagonal_imaginary / modulus])


def operate(padded, mach_field, grid_level):
    centre = padded[:, 1:-1, 1:-1, 1:-1]
    east_cells = padded[:, 2:, 1:-1, 1:-1]
    west_cells = padded[:, :-2, 1:-1, 1:-1]
    north_cells = padded[:, 1:-1, 2:, 1:-1]
    south_cells = padded[:, 1:-1, :-2, 1:-1]
    upper_cells = padded[:, 1:-1, 1:-1, 2:]
    lower_cells = padded[:, 1:-1, 1:-1, :-2]
    diffusion_scale = 0.25 ** grid_level
    axial_weight = 1.0 - mach_field * mach_field
    spread = diffusion_scale * (axial_weight * (2.0 * centre - east_cells - west_cells)
                                + (2.0 * centre - north_cells - south_cells)
                                + (2.0 * centre - upper_cells - lower_cells))
    advect = wave_step * 0.5 ** grid_level * mach_field
    axial_slope = east_cells - west_cells
    wave_square = wave_step * wave_step
    real_part = spread[0] + advect * axial_slope[1] - wave_square * (centre[0] + 0.5 * centre[1])
    imaginary = spread[1] - advect * axial_slope[0] - wave_square * (centre[1] - 0.5 * centre[0])
    return jnp.stack([real_part, imaginary])


def jacobi_step(solution, padded, source, mach_field, inverse, grid_level):
    return solution + jacobi_weight * complex_times(source - operate(padded, mach_field, grid_level), inverse)


def restrict(values):
    leading = values.shape[:-3]
    leading_rank = len(leading)
    first_length, second_length, third_length = values.shape[-3:]
    grouped = values.reshape(leading + (first_length // 2, 2, second_length // 2, 2, third_length // 2, 2))
    return grouped.mean(axis=(leading_rank + 1, leading_rank + 3, leading_rank + 5))


def prolong(values):
    leading = values.shape[:-3]
    first_length, second_length, third_length = values.shape[-3:]
    expanded = values[..., :, None, :, None, :, None]
    expanded = jnp.broadcast_to(expanded, leading + (first_length, 2, second_length, 2, third_length, 2))
    return expanded.reshape(leading + (2 * first_length, 2 * second_length, 2 * third_length))


def pad_cells(solution):
    return jnp.pad(solution, ((0, 0), (1, 1), (1, 1), (1, 1)))


def coarse_solve(source, mach_field, grid_level):
    inverse = inverse_diagonal(mach_field, grid_level)
    solution = jacobi_weight * complex_times(source, inverse)
    for sweep_index in range(COARSE_SWEEPS - 1):
        solution = jacobi_step(solution, pad_cells(solution), source, mach_field, inverse, grid_level)
    return solution


def multigrid(source, mach_levels, grid_level):
    mach_field = mach_levels[grid_level]
    if grid_level == LEVELS - 1:
        return coarse_solve(source, mach_field, grid_level)
    inverse = inverse_diagonal(mach_field, grid_level)
    solution = jacobi_weight * complex_times(source, inverse)
    for sweep_index in range(PRE - 1):
        solution = jacobi_step(solution, pad_cells(solution), source, mach_field, inverse, grid_level)
    residual = source - operate(pad_cells(solution), mach_field, grid_level)
    coarse = multigrid(restrict(residual), mach_levels, grid_level + 1)
    solution = solution + prolong(coarse)
    for sweep_index in range(POST):
        solution = jacobi_step(solution, pad_cells(solution), source, mach_field, inverse, grid_level)
    return solution


def reference(source_field, mach_number):
    mach_levels = [mach_number.astype(jnp.float32)]
    for grid_level in range(1, LEVELS):
        mach_levels.append(restrict(mach_levels[-1]))
    return multigrid(source_field, mach_levels, 0)
```

```python
import functools

import jax
import jax.numpy as jnp
from jax import lax
from jax.experimental import pallas as pl
from jax.experimental.pallas import tpu as pltpu
from jax.sharding import PartitionSpec as P

MESH = pl.DeviceIdType.MESH
AXES = ("gx", "gy", "gz")
COARSE_SWEEPS = 6
WAVE = 0.25
WAVE2 = 0.0625
LANES = 128


def lane_of(shape):
    return lax.broadcasted_iota(jnp.int32, shape, len(shape) - 1)


def row_of(shape):
    return lax.broadcasted_iota(jnp.int32, shape, len(shape) - 2)


def roll(value, shift, axis):
    if isinstance(shift, int):
        shift %= value.shape[axis]
        if shift == 0:
            return value
    return pltpu.roll(value, shift, axis)


def coefficients(mach, level):
    scale = 0.25**level
    axial = scale * (1.0 - mach * mach)
    real = 2.0 * axial + (4.0 * scale - WAVE2)
    imaginary = 0.5 * WAVE2
    half = 0.5 / (real * real + imaginary * imaginary)
    return axial, real * half, -imaginary * half


def pair_sum(value, rows, lanes):
    shape = value.shape
    even = (row_of(shape) // rows) % 2 == 0
    value = value + jnp.where(even, roll(value, shape[0] - rows, 0), roll(value, rows, 0))
    even = (lane_of(shape) // lanes) % 2 == 0
    return value + jnp.where(even, roll(value, LANES - lanes, 1), roll(value, lanes, 1))


def kernel(sizes, g0, mach_in, out, v0, v1, gl1, co0, co1, ys0, yr0, ys1, yr1, zs, zr, gm, gg,
           va, vb, vc, gc2, gc3, gc4, cc2, cc3, cc4, own, send_sem, recv_sem, gs_sem, gr_sem):
    nx, ny, nz = sizes
    count = nx * ny * nz
    ix, iy, iz = (lax.axis_index(a) for a in AXES)
    me = (ix * ny + iy) * nz + iz
    X0, Y0 = g0.shape[1], g0.shape[2]
    tile = (Y0, LANES)
    here = {"gx": ix, "gy": iy, "gz": iz}
    size = dict(zip(AXES, sizes))
    yall = va.shape[3]
    XC = X0 // 4

    def peer(d):
        t = lax.rem(me + d, count)
        return (t // (ny * nz), lax.rem(t // nz, ny), lax.rem(t, nz))

    barrier = pltpu.get_barrier_semaphore()

    def greet(d, carry):
        pl.semaphore_signal(barrier, inc=1, device_id=peer(d), device_id_type=MESH)
        return carry

    for ref in (v0, v1):
        zero = jnp.zeros((2,) + tile, jnp.float32)
        for r in range(4):
            ref[r, :, 0] = zero
            ref[r, :, ref.shape[2] - 1] = zero
    yr0[...] = jnp.zeros(yr0.shape, jnp.float32)
    yr1[...] = jnp.zeros(yr1.shape, jnp.float32)
    zr[...] = jnp.zeros(zr.shape, jnp.float32)
    lax.fori_loop(1, count, greet, 0)

    lane, row = lane_of(tile), row_of(tile)
    levels = (
        dict(v=v0, g=g0, co=co0, ys=ys0, yr=yr0, X=X0, w=1, l=0),
        dict(v=v1, g=gl1, co=co1, ys=ys1, yr=yr1, X=X0 // 2, w=2, l=1),
    )

    def links(L, r):
        X, v, ys, yr = L["X"], L["v"].at[r], L["ys"].at[r], L["yr"].at[r]
        k = 4 * L["l"] + r
        pieces = []
        for n, (axis, step, src, dst) in enumerate((
            ("gz", 1, zs.at[k], zr.at[k, 0]),
            ("gz", -1, zs.at[k], zr.at[k, 1]),
            ("gy", 1, ys.at[1], yr.at[0]),
            ("gy", -1, ys.at[0], yr.at[1]),
            ("gx", 1, v.at[:, X], v.at[:, 0]),
            ("gx", -1, v.at[:, 1], v.at[:, X + 1]),
        )):
            at = here[axis]
            up, down = at < size[axis] - 1, at > 0
            to = tuple(here[a] + step if a == axis else here[a] for a in AXES)
            copy = pltpu.make_async_remote_copy(
                src_ref=src, dst_ref=dst, send_sem=send_sem.at[k, n], recv_sem=recv_sem.at[k, n],
                device_id=to, device_id_type=MESH,
            )
            pieces.append((copy, up if step > 0 else down, down if step > 0 else up))
        return pieces

    def start(L, r):
        for copy, sends, _ in links(L, r):
            pl.when(sends)(copy.start)

    def arrive(L, r):
        for copy, _, receives in links(L, r):
            pl.when(receives)(copy.wait_recv)

    def sent(L, r):
        for copy, sends, _ in links(L, r):
            pl.when(sends)(copy.wait_send)

    def put(L, r, x, values, packed):
        v, ys = L["v"], L["ys"]
        for c in range(2):
            value = values[c]
            v[r, c, x + 1] = value
            ys[r, 0, c, pl.ds(x, 1), :] = value[:1]
            ys[r, 1, c, pl.ds(x, 1), :] = value[Y0 - 1:]
            packed = jnp.where(lane // 4 == x + 16 * c, roll(value, 4 * x + 2 + 64 * c, 1), packed)
        return packed

    def seal(L, r, packed):
        zs[4 * L["l"] + r] = packed
        start(L, r)

    def sides(L, r):
        k, w = 4 * L["l"] + r, L["w"]
        below = (lane % 4 >= 2 - w) & (lane % 4 < 2)
        return jnp.where(below, zr[k, 0], roll(zr[k, 1], LANES - 2 * w, 1))

    def terms(L, r, x, side):
        v, yr, w, co = L["v"], L["yr"], L["w"], L["co"]
        scale = 0.25 ** L["l"]
        axial, drift = co[0, x], co[3, x]
        centre, along, across = [], [], []
        slope = []
        for c in range(2):
            here_ = v[r, c, x + 1]
            east, west = v[r, c, x + 2], v[r, c, x]
            shift = lax.rem(4 * LANES - (4 * x + 2 - w + 64 * c), LANES)
            edge = roll(side, shift, 1)
            lower = jnp.where(lane < w, edge, roll(here_, w, 1))
            upper = jnp.where(lane >= LANES - w, edge, roll(here_, LANES - w, 1))
            south = jnp.where(row < w, yr[r, 0, c, pl.ds(x, 1), :], roll(here_, w, 0))
            north = jnp.where(row >= Y0 - w, yr[r, 1, c, pl.ds(x, 1), :], roll(here_, Y0 - w, 0))
            centre.append(here_)
            across.append((lower + upper) + (south + north))
            along.append(east + west)
            slope.append(east - west)
        if L["l"]:
            across = [scale * a for a in across]
        g = L["g"]
        real = g[0, x] + axial * along[0] + across[0] - drift * slope[1]
        imaginary = g[1, x] + axial * along[1] + across[1] + drift * slope[0]
        return centre, (real, imaginary)

    def relaxed(centre, t, hr, hi):
        return (0.5 * centre[0] + (hr * t[0] - hi * t[1]), 0.5 * centre[1] + (hi * t[0] + hr * t[1]))

    def residue(centre, t, axial, scale):
        dr = 2.0 * axial + (4.0 * scale - WAVE2)
        di = 0.5 * WAVE2
        return (t[0] - dr * centre[0] + di * centre[1], t[1] - dr * centre[1] - di * centre[0])

    def relax(L, r):
        arrive(L, r)
        side = sides(L, r)
        co = L["co"]

        def body(x, packed):
            centre, t = terms(L, r, x, side)
            return put(L, r + 1, x, relaxed(centre, t, co[1, x], co[2, x]), packed)

        seal(L, r + 1, lax.fori_loop(0, L["X"], body, jnp.zeros(tile, jnp.float32), unroll=4))

    def last(L, r, store):
        arrive(L, r)
        side = sides(L, r)
        co = L["co"]

        def body(x, carry):
            centre, t = terms(L, r, x, side)
            store(x, relaxed(centre, t, co[1, x], co[2, x]))
            return carry

        lax.fori_loop(0, L["X"], body, 0, unroll=4)

    def residual(L, r, x, side):
        centre, t = terms(L, r, x, side)
        return residue(centre, t, L["co"][0, x], 0.25 ** L["l"])

    def set_coefficients(co, x, mach, level):
        axial, hr, hi = coefficients(mach, level)
        co[0, x] = axial
        co[1, x] = hr
        co[2, x] = hi
        co[3, x] = (WAVE * 0.5**level) * mach
        return hr, hi

    def first(hr, hi, gr, gi):
        return hr * gr - hi * gi, hr * gi + hi * gr

    fine, half = levels

    def open_plane(x, packed):
        mach = mach_in[x].astype(jnp.float32)
        hr, hi = set_coefficients(co0, x, mach, 0)
        return put(fine, 0, x, first(hr, hi, g0[0, x], g0[1, x]), packed)

    packed = lax.fori_loop(0, X0, open_plane, jnp.zeros(tile, jnp.float32), unroll=4)

    def mach_plane(x, carry):
        mach = mach_in[2 * x].astype(jnp.float32) + mach_in[2 * x + 1].astype(jnp.float32)
        set_coefficients(co1, x, 0.125 * pair_sum(mach, 1, 1), 1)
        return carry

    pl.semaphore_wait(barrier, count - 1)
    seal(fine, 0, packed)

    lax.fori_loop(0, X0 // 2, mach_plane, 0, unroll=2)
    undo = 1.0 / (WAVE * 0.5)
    group = jnp.zeros(tile, jnp.float32)
    for x in range(XC):
        mach = pair_sum((co1[3, 2 * x] + co1[3, 2 * x + 1]) * undo, 2, 2) * 0.125
        group = jnp.where(lane % 4 == x, mach, group)
    for y in range(4):
        gm[me, y:y + 1, :] = group[4 * y:4 * y + 1]
        gm[me, y + 4:y + 5, :] = group[4 * y:4 * y + 1]

    def tell(ref, n):
        def one(d, carry):
            pltpu.make_async_remote_copy(
                src_ref=ref.at[me], dst_ref=ref.at[me], send_sem=gs_sem.at[n], recv_sem=gr_sem.at[n],
                device_id=peer(d), device_id_type=MESH,
            ).start()
            return carry

        lax.fori_loop(1, count, one, 0)

    def bulk(ref, n):
        part = ref.at[pl.ds(0, count - 1)]
        return pltpu.make_async_remote_copy(
            src_ref=part, dst_ref=part, send_sem=gs_sem.at[n], recv_sem=gr_sem.at[n],
            device_id=peer(1), device_id_type=MESH,
        )

    def spread(ref, store):
        lane8 = lane_of((8, LANES))

        def block(bx, carry):
            for by in range(ny):
                tiles = [ref[(bx * ny + by) * nz + bz] for bz in range(nz)]
                for x in range(XC):
                    value = tiles[0]
                    for bz in range(nz):
                        moved = roll(tiles[bz], bz - x, 1)
                        value = moved if bz == 0 else jnp.where(lane8 % 4 == bz, moved, value)
                    store(bx * XC + x, by, value)
            return carry

        lax.fori_loop(0, nx, block, 0)

    tell(gm, 0)

    wide = (yall, LANES)
    clane, crow = lane_of(wide), row_of(wide)
    coarse = (
        dict(v=va, g=gc2, co=cc2, w=1, l=2),
        dict(v=vb, g=gc3, co=cc3, w=2, l=3),
        dict(v=vc, g=gc4, co=cc4, w=4, l=4),
    )
    for C in coarse:
        v = C["v"]
        C["X"] = v.shape[2] - 2
        C["unroll"] = min(4, C["X"])
        for r in range(2):
            for c in range(2):
                v[r, c, 0] = jnp.zeros(wide, jnp.float32)
                v[r, c, C["X"] + 1] = jnp.zeros(wide, jnp.float32)

    def over(C, body):
        def step(x, carry):
            body(x)
            return carry

        lax.fori_loop(0, C["X"], step, 0, unroll=C["unroll"])

    def coarse_terms(C, r, x):
        v, w, co, g = C["v"], C["w"], C["co"], C["g"]
        m = 4 * w
        scale = 0.25 ** C["l"]
        top = clane >= LANES - m
        centre, along, across, slope = [], [], [], []
        for c in range(2):
            value = v[r, c, x + 1]
            east, west = v[r, c, x + 2], v[r, c, x]
            upper = jnp.where(top, roll(value, LANES - m - 1, 1), roll(value, LANES - m, 1))
            upper = jnp.where(top & (clane % 4 == 3), 0.0, upper)
            lower = jnp.where(clane < m, roll(value, m + 1, 1), roll(value, m, 1))
            lower = jnp.where((clane < m) & (clane % 4 == 0), 0.0, lower)
            south = jnp.where(crow < w, 0.0, roll(value, w, 0))
            north = jnp.where(crow >= yall - w, 0.0, roll(value, yall - w, 0))
            centre.append(value)
            across.append(scale * ((lower + upper) + (south + north)))
            along.append(east + west)
            slope.append(east - west)
        real = g[0, x] + co[0, x] * along[0] + across[0] - co[3, x] * slope[1]
        imaginary = g[1, x] + co[0, x] * along[1] + across[1] + co[3, x] * slope[0]
        return centre, (real, imaginary)

    def coarse_first(C):
        def body(x):
            g, co = C["g"], C["co"]
            values = first(co[1, x], co[2, x], g[0, x], g[1, x])
            for c in range(2):
                C["v"][0, c, x + 1] = values[c]

        over(C, body)

    def coarse_relax(C, r):
        def body(x):
            centre, t = coarse_terms(C, r, x)
            values = relaxed(centre, t, C["co"][1, x], C["co"][2, x])
            for c in range(2):
                C["v"][1 - r, c, x + 1] = values[c]

        over(C, body)

    def coarse_down(C, D, r):
        w = C["w"]

        def body(x):
            total = None
            for half_ in range(2):
                centre, t = coarse_terms(C, r, 2 * x + half_)
                res = residue(centre, t, C["co"][0, 2 * x + half_], 0.25 ** C["l"])
                total = res if total is None else tuple(a + b for a, b in zip(total, res))
            for c in range(2):
                D["g"][c, x] = 0.125 * pair_sum(total[c], w, 4 * w)

        over(D, body)

    def coarse_up(C, D, r, rd):
        def body(x):
            for c in range(2):
                add = D["v"][rd, c, x + 1]
                for half_ in range(2):
                    C["v"][r, c, 2 * x + half_ + 1] = C["v"][r, c, 2 * x + half_ + 1] + add

        over(D, body)

    relax(fine, 0)
    arrive(fine, 1)
    side = sides(fine, 1)

    def down_plane(x, packed):
        a = residual(fine, 1, 2 * x, side)
        b = residual(fine, 1, 2 * x + 1, side)
        g = [0.125 * pair_sum(a[c] + b[c], 1, 1) for c in range(2)]
        for c in range(2):
            gl1[c, x] = g[c]
        return put(half, 0, x, first(co1[1, x], co1[2, x], g[0], g[1]), packed)

    packed = lax.fori_loop(0, X0 // 2, down_plane, jnp.zeros(tile, jnp.float32), unroll=2)
    seal(half, 0, packed)

    bulk(gm, 0).wait_recv()

    def store_mach(x, by, value):
        cc2[3, x, 4 * by:4 * by + 4, :] = value[:4]

    spread(gm, store_mach)
    over(coarse[0], lambda x: set_coefficients(cc2, x, cc2[3, x], 2))
    for C, D in zip(coarse[:-1], coarse[1:]):
        factor = 0.125 / (WAVE * 0.5 ** C["l"])

        def body(x, C=C, D=D, factor=factor):
            mach = factor * pair_sum(C["co"][3, 2 * x] + C["co"][3, 2 * x + 1], C["w"], 4 * C["w"])
            set_coefficients(D["co"], x, mach, D["l"])

        over(D, body)

    relax(half, 0)
    arrive(half, 1)
    side = sides(half, 1)
    groups = [jnp.zeros(tile, jnp.float32) for _ in range(2)]
    for x in range(XC):
        a = residual(half, 1, 2 * x, side)
        b = residual(half, 1, 2 * x + 1, side)
        for c in range(2):
            groups[c] = jnp.where(lane % 4 == x, 0.125 * pair_sum(a[c] + b[c], 2, 2), groups[c])
    for c in range(2):
        for y in range(4):
            gg[me, 4 * c + y:4 * c + y + 1, :] = groups[c][4 * y:4 * y + 1]
    tell(gg, 1)
    bulk(gg, 1).wait_recv()

    def store_source(x, by, value):
        for c in range(2):
            gc2[c, x, 4 * by:4 * by + 4, :] = value[4 * c:4 * c + 4]

    spread(gg, store_source)

    for C, D in zip(coarse[:-1], coarse[1:]):
        coarse_first(C)
        coarse_relax(C, 0)
        coarse_down(C, D, 1)
    coarse_first(coarse[2])
    at = 0
    for _ in range(COARSE_SWEEPS - 1):
        coarse_relax(coarse[2], at)
        at = 1 - at
    for C, D in ((coarse[1], coarse[2]), (coarse[0], coarse[1])):
        coarse_up(C, D, 1, at)
        coarse_relax(C, 1)
        coarse_relax(C, 0)
        at = 1

    packed = jnp.zeros(tile, jnp.float32)
    for x in range(XC):
        for c in range(2):
            value = va[1, c, ix * XC + x + 1]
            only = jnp.where(clane % 4 == iz, value, 0.0)
            back = only + roll(only, 1, 1)
            back = back + roll(back, 2, 1)
            ahead = only + roll(only, LANES - 1, 1)
            ahead = ahead + roll(ahead, LANES - 2, 1)
            own[c, x] = jnp.where(clane % 4 <= iz, ahead, back)
    for x in range(XC):
        add = []
        for c in range(2):
            value = own[c, x, pl.ds(4 * iy, 1), :]
            full = jnp.broadcast_to(value, tile)
            for y in range(1, 4):
                value = own[c, x, pl.ds(4 * iy + y, 1), :]
                full = jnp.where(row >= 4 * y, value, full)
            add.append(full)
        for half_ in range(2):
            values = [v1[1, c, 2 * x + half_ + 1] + add[c] for c in range(2)]
            packed = put(half, 2, 2 * x + half_, values, packed)
    seal(half, 2, packed)
    relax(half, 2)

    def store_half(x, values):
        for c in range(2):
            gl1[c, x] = values[c]

    last(half, 3, store_half)

    def up_plane(x, packed):
        values = [v0[1, c, x + 1] + gl1[c, x // 2] for c in range(2)]
        return put(fine, 2, x, values, packed)

    seal(fine, 2, lax.fori_loop(0, X0, up_plane, jnp.zeros(tile, jnp.float32), unroll=4))
    relax(fine, 2)

    def store_out(x, values):
        for c in range(2):
            out[c, x] = values[c]

    last(fine, 3, store_out)

    for r in range(4):
        sent(fine, r)
        sent(half, r)
    bulk(gm, 0).wait_send()
    bulk(gg, 1).wait_send()


def solution(mesh):
    sizes = tuple(mesh.shape[a] for a in AXES)
    nx, ny, nz = sizes
    count = nx * ny * nz

    def shards(source, mach):
        _, X, Y, Z = source.shape
        assert X == 16 and Y == 16 and Z == LANES and nz == 4, "unsupported sizes"
        f32 = jnp.float32
        yall = ny * Y // 4
        xs = [nx * X // 2**l for l in (2, 3, 4)]
        scratch = [
            pltpu.VMEM((4, 2, X + 2, Y, LANES), f32),
            pltpu.VMEM((4, 2, X // 2 + 2, Y, LANES), f32),
            pltpu.VMEM((2, X // 2, Y, LANES), f32),
            pltpu.VMEM((4, X, Y, LANES), f32),
            pltpu.VMEM((4, X // 2, Y, LANES), f32),
            pltpu.VMEM((4, 2, 2, X, LANES), f32),
            pltpu.VMEM((4, 2, 2, X, LANES), f32),
            pltpu.VMEM((4, 2, 2, X // 2, LANES), f32),
            pltpu.VMEM((4, 2, 2, X // 2, LANES), f32),
            pltpu.VMEM((8, Y, LANES), f32),
            pltpu.VMEM((8, 2, Y, LANES), f32),
            pltpu.VMEM((count, 8, LANES), f32),
            pltpu.VMEM((count, 8, LANES), f32),
        ]
        scratch += [pltpu.VMEM((2, 2, n + 2, yall, LANES), f32) for n in xs]
        scratch += [pltpu.VMEM((2, n, yall, LANES), f32) for n in xs]
        scratch += [pltpu.VMEM((4, n, yall, LANES), f32) for n in xs]
        scratch += [
            pltpu.VMEM((2, X // 4, yall, LANES), f32),
            pltpu.SemaphoreType.DMA((8, 6)),
            pltpu.SemaphoreType.DMA((8, 6)),
            pltpu.SemaphoreType.DMA((2,)),
            pltpu.SemaphoreType.DMA((2,)),
        ]
        return pl.pallas_call(
            functools.partial(kernel, sizes),
            out_shape=jax.ShapeDtypeStruct(source.shape, f32),
            in_specs=[pl.BlockSpec(memory_space=pltpu.VMEM)] * 2,
            out_specs=pl.BlockSpec(memory_space=pltpu.VMEM),
            scratch_shapes=scratch,
            compiler_params=pltpu.CompilerParams(
                collective_id=0, has_side_effects=True, vmem_limit_bytes=48 * 2**20
            ),
        )(source, mach)

    return jax.shard_map(
        shards,
        mesh=mesh,
        in_specs=(P(None, "gx", "gy", "gz"), P("gx", "gy", "gz")),
        out_specs=P(None, "gx", "gy", "gz"),
        check_vma=False,
    )
```

```python
import functools

import jax
import jax.numpy as jnp
from jax import lax
from jax.experimental import pallas as pl
from jax.experimental.pallas import tpu as pltpu
from jax.sharding import PartitionSpec as P

MESH = pl.DeviceIdType.MESH
AXES = ("gx", "gy", "gz")
COARSE_SWEEPS = 6
WAVE = 0.25
WAVE2 = 0.0625
LANES = 128


def lane_of(shape):
    return lax.broadcasted_iota(jnp.int32, shape, len(shape) - 1)


def row_of(shape):
    return lax.broadcasted_iota(jnp.int32, shape, len(shape) - 2)


def roll(value, shift, axis):
    if isinstance(shift, int):
        shift %= value.shape[axis]
        if shift == 0:
            return value
    return pltpu.roll(value, shift, axis)


def coefficients(mach, level):
    scale = 0.25**level
    axial = scale * (1.0 - mach * mach)
    real = 2.0 * axial + (4.0 * scale - WAVE2)
    imaginary = 0.5 * WAVE2
    half = 0.5 / (real * real + imaginary * imaginary)
    return axial, real * half, -imaginary * half


def pair_sum(value, rows, lanes):
    shape = value.shape
    even = (row_of(shape) // rows) % 2 == 0
    value = value + jnp.where(even, roll(value, shape[0] - rows, 0), roll(value, rows, 0))
    even = (lane_of(shape) // lanes) % 2 == 0
    return value + jnp.where(even, roll(value, LANES - lanes, 1), roll(value, lanes, 1))


def kernel(sizes, g_hbm, mach_hbm, out, g0, mach_in, in_sem, v0, v1, gl1, co0, co1, ys0, yr0, ys1, yr1, zs, zr, gm, gg,
           va, vb, vc, gc2, gc3, gc4, cc2, cc3, cc4, own, send_sem, recv_sem, gs_sem, gr_sem):
    nx, ny, nz = sizes
    count = nx * ny * nz
    ix, iy, iz = (lax.axis_index(a) for a in AXES)
    me = (ix * ny + iy) * nz + iz
    X0, Y0 = g0.shape[1], g0.shape[2]
    tile = (Y0, LANES)
    here = {"gx": ix, "gy": iy, "gz": iz}
    size = dict(zip(AXES, sizes))
    yall = va.shape[3]
    XC = X0 // 4

    def peer(d):
        t = lax.rem(me + d, count)
        return (t // (ny * nz), lax.rem(t // nz, ny), lax.rem(t, nz))

    loads = [
        pltpu.make_async_copy(mach_hbm, mach_in, in_sem.at[0]),
        pltpu.make_async_copy(g_hbm, g0, in_sem.at[1]),
    ]
    for load in loads:
        load.start()
    barrier = pltpu.get_barrier_semaphore()

    def greet(d, carry):
        pl.semaphore_signal(barrier, inc=1, device_id=peer(d), device_id_type=MESH)
        return carry

    for ref in (v0, v1):
        zero = jnp.zeros((2,) + tile, jnp.float32)
        for r in range(4):
            ref[r, :, 0] = zero
            ref[r, :, ref.shape[2] - 1] = zero
    yr0[...] = jnp.zeros(yr0.shape, jnp.float32)
    yr1[...] = jnp.zeros(yr1.shape, jnp.float32)
    zr[...] = jnp.zeros(zr.shape, jnp.float32)
    lax.fori_loop(1, count, greet, 0)

    lane, row = lane_of(tile), row_of(tile)
    levels = (
        dict(v=v0, g=g0, co=co0, ys=ys0, yr=yr0, X=X0, w=1, l=0),
        dict(v=v1, g=gl1, co=co1, ys=ys1, yr=yr1, X=X0 // 2, w=2, l=1),
    )

    def links(L, r):
        X, v, ys, yr = L["X"], L["v"].at[r], L["ys"].at[r], L["yr"].at[r]
        k = 4 * L["l"] + r
        pieces = []
        for n, (axis, step, src, dst) in enumerate((
            ("gz", 1, zs.at[k], zr.at[k, 0]),
            ("gz", -1, zs.at[k], zr.at[k, 1]),
            ("gy", 1, ys.at[1], yr.at[0]),
            ("gy", -1, ys.at[0], yr.at[1]),
            ("gx", 1, v.at[:, X], v.at[:, 0]),
            ("gx", -1, v.at[:, 1], v.at[:, X + 1]),
        )):
            at = here[axis]
            up, down = at < size[axis] - 1, at > 0
            to = tuple(here[a] + step if a == axis else here[a] for a in AXES)
            copy = pltpu.make_async_remote_copy(
                src_ref=src, dst_ref=dst, send_sem=send_sem.at[k, n], recv_sem=recv_sem.at[k, n],
                device_id=to, device_id_type=MESH,
            )
            pieces.append((copy, up if step > 0 else down, down if step > 0 else up))
        return pieces

    def start(L, r):
        for copy, sends, _ in links(L, r):
            pl.when(sends)(copy.start)

    flying = []

    def arrive(L, r):
        for earlier in flying:
            sent(*earlier)
        flying[:] = [(L, r)]
        for copy, _, receives in links(L, r):
            pl.when(receives)(copy.wait_recv)

    def sent(L, r):
        for copy, sends, _ in links(L, r):
            pl.when(sends)(copy.wait_send)

    def put(L, r, x, values, packed):
        v, ys = L["v"], L["ys"]
        for c in range(2):
            value = values[c]
            v[r, c, x + 1] = value
            ys[r, 0, c, pl.ds(x, 1), :] = value[:1]
            ys[r, 1, c, pl.ds(x, 1), :] = value[Y0 - 1:]
            packed = jnp.where(lane // 4 == x + 16 * c, roll(value, 4 * x + 2 + 64 * c, 1), packed)
        return packed

    def seal(L, r, packed):
        zs[4 * L["l"] + r] = packed
        start(L, r)

    def sides(L, r):
        k, w = 4 * L["l"] + r, L["w"]
        below = (lane % 4 >= 2 - w) & (lane % 4 < 2)
        return jnp.where(below, zr[k, 0], roll(zr[k, 1], LANES - 2 * w, 1))

    def terms(L, r, x, side):
        v, yr, w, co = L["v"], L["yr"], L["w"], L["co"]
        scale = 0.25 ** L["l"]
        axial, drift = co[0, x], co[3, x]
        centre, along, across = [], [], []
        slope = []
        for c in range(2):
            here_ = v[r, c, x + 1]
            east, west = v[r, c, x + 2], v[r, c, x]
            shift = lax.rem(4 * LANES - (4 * x + 2 - w + 64 * c), LANES)
            edge = roll(side, shift, 1)
            lower = jnp.where(lane < w, edge, roll(here_, w, 1))
            upper = jnp.where(lane >= LANES - w, edge, roll(here_, LANES - w, 1))
            south = jnp.where(row < w, yr[r, 0, c, pl.ds(x, 1), :], roll(here_, w, 0))
            north = jnp.where(row >= Y0 - w, yr[r, 1, c, pl.ds(x, 1), :], roll(here_, Y0 - w, 0))
            centre.append(here_)
            across.append((lower + upper) + (south + north))
            along.append(east + west)
            slope.append(east - west)
        if L["l"]:
            across = [scale * a for a in across]
        g = L["g"]
        real = g[0, x] + axial * along[0] + across[0] - drift * slope[1]
        imaginary = g[1, x] + axial * along[1] + across[1] + drift * slope[0]
        return centre, (real, imaginary)

    def relaxed(centre, t, hr, hi):
        return (0.5 * centre[0] + (hr * t[0] - hi * t[1]), 0.5 * centre[1] + (hi * t[0] + hr * t[1]))

    def residue(centre, t, axial, scale):
        dr = 2.0 * axial + (4.0 * scale - WAVE2)
        di = 0.5 * WAVE2
        return (t[0] - dr * centre[0] + di * centre[1], t[1] - dr * centre[1] - di * centre[0])

    def relax(L, r):
        arrive(L, r)
        side = sides(L, r)
        co = L["co"]

        def body(x, packed):
            centre, t = terms(L, r, x, side)
            return put(L, r + 1, x, relaxed(centre, t, co[1, x], co[2, x]), packed)

        seal(L, r + 1, lax.fori_loop(0, L["X"], body, jnp.zeros(tile, jnp.float32), unroll=True))

    def last(L, r, store):
        arrive(L, r)
        side = sides(L, r)
        co = L["co"]

        def body(x, carry):
            centre, t = terms(L, r, x, side)
            store(x, relaxed(centre, t, co[1, x], co[2, x]))
            return carry

        lax.fori_loop(0, L["X"], body, 0, unroll=True)

    def residual(L, r, x, side):
        centre, t = terms(L, r, x, side)
        return residue(centre, t, L["co"][0, x], 0.25 ** L["l"])

    def set_coefficients(co, x, mach, level):
        axial, hr, hi = coefficients(mach, level)
        co[0, x] = axial
        co[1, x] = hr
        co[2, x] = hi
        co[3, x] = (WAVE * 0.5**level) * mach
        return hr, hi

    def first(hr, hi, gr, gi):
        return hr * gr - hi * gi, hr * gi + hi * gr

    fine, half = levels

    def open_plane(x, packed):
        mach = mach_in[x].astype(jnp.float32)
        hr, hi = set_coefficients(co0, x, mach, 0)
        return put(fine, 0, x, first(hr, hi, g0[0, x], g0[1, x]), packed)

    for load in loads:
        load.wait()
    packed = lax.fori_loop(0, X0, open_plane, jnp.zeros(tile, jnp.float32), unroll=True)

    def mach_plane(x, carry):
        mach = mach_in[2 * x].astype(jnp.float32) + mach_in[2 * x + 1].astype(jnp.float32)
        set_coefficients(co1, x, 0.125 * pair_sum(mach, 1, 1), 1)
        return carry

    pl.semaphore_wait(barrier, count - 1)
    seal(fine, 0, packed)

    lax.fori_loop(0, X0 // 2, mach_plane, 0, unroll=True)
    undo = 1.0 / (WAVE * 0.5)
    group = jnp.zeros(tile, jnp.float32)
    for x in range(XC):
        mach = pair_sum((co1[3, 2 * x] + co1[3, 2 * x + 1]) * undo, 2, 2) * 0.125
        group = jnp.where(lane % 4 == x, mach, group)
    for y in range(4):
        gm[me, y:y + 1, :] = group[4 * y:4 * y + 1]
        gm[me, y + 4:y + 5, :] = group[4 * y:4 * y + 1]

    def tell(ref, n):
        def one(d, carry):
            pltpu.make_async_remote_copy(
                src_ref=ref.at[me], dst_ref=ref.at[me], send_sem=gs_sem.at[n], recv_sem=gr_sem.at[n],
                device_id=peer(d), device_id_type=MESH,
            ).start()
            return carry

        lax.fori_loop(1, count, one, 0)

    def bulk(ref, n):
        part = ref.at[pl.ds(0, count - 1)]
        return pltpu.make_async_remote_copy(
            src_ref=part, dst_ref=part, send_sem=gs_sem.at[n], recv_sem=gr_sem.at[n],
            device_id=peer(1), device_id_type=MESH,
        )

    def spread(ref, store):
        lane8 = lane_of((8, LANES))

        def block(bx, carry):
            for by in range(ny):
                tiles = [ref[(bx * ny + by) * nz + bz] for bz in range(nz)]
                for x in range(XC):
                    value = tiles[0]
                    for bz in range(nz):
                        moved = roll(tiles[bz], bz - x, 1)
                        value = moved if bz == 0 else jnp.where(lane8 % 4 == bz, moved, value)
                    store(bx * XC + x, by, value)
            return carry

        lax.fori_loop(0, nx, block, 0, unroll=True if nx <= 4 else 1)

    tell(gm, 0)

    wide = (yall, LANES)
    clane, crow = lane_of(wide), row_of(wide)
    coarse = (
        dict(v=va, g=gc2, co=cc2, w=1, l=2),
        dict(v=vb, g=gc3, co=cc3, w=2, l=3),
        dict(v=vc, g=gc4, co=cc4, w=4, l=4),
    )
    for C in coarse:
        v = C["v"]
        C["X"] = v.shape[2] - 2
        C["unroll"] = True if C["X"] <= 16 else 4
        for r in range(2):
            for c in range(2):
                v[r, c, 0] = jnp.zeros(wide, jnp.float32)
                v[r, c, C["X"] + 1] = jnp.zeros(wide, jnp.float32)

    def over(C, body):
        def step(x, carry):
            body(x)
            return carry

        lax.fori_loop(0, C["X"], step, 0, unroll=C["unroll"])

    def coarse_terms(C, r, x):
        v, w, co, g = C["v"], C["w"], C["co"], C["g"]
        m = 4 * w
        scale = 0.25 ** C["l"]
        top = clane >= LANES - m
        centre, along, across, slope = [], [], [], []
        for c in range(2):
            value = v[r, c, x + 1]
            east, west = v[r, c, x + 2], v[r, c, x]
            upper = jnp.where(top, roll(value, LANES - m - 1, 1), roll(value, LANES - m, 1))
            upper = jnp.where(top & (clane % 4 == 3), 0.0, upper)
            lower = jnp.where(clane < m, roll(value, m + 1, 1), roll(value, m, 1))
            lower = jnp.where((clane < m) & (clane % 4 == 0), 0.0, lower)
            south = jnp.where(crow < w, 0.0, roll(value, w, 0))
            north = jnp.where(crow >= yall - w, 0.0, roll(value, yall - w, 0))
            centre.append(value)
            across.append(scale * ((lower + upper) + (south + north)))
            along.append(east + west)
            slope.append(east - west)
        real = g[0, x] + co[0, x] * along[0] + across[0] - co[3, x] * slope[1]
        imaginary = g[1, x] + co[0, x] * along[1] + across[1] + co[3, x] * slope[0]
        return centre, (real, imaginary)

    def coarse_first(C):
        def body(x):
            g, co = C["g"], C["co"]
            values = first(co[1, x], co[2, x], g[0, x], g[1, x])
            for c in range(2):
                C["v"][0, c, x + 1] = values[c]

        over(C, body)

    def coarse_relax(C, r):
        def body(x):
            centre, t = coarse_terms(C, r, x)
            values = relaxed(centre, t, C["co"][1, x], C["co"][2, x])
            for c in range(2):
                C["v"][1 - r, c, x + 1] = values[c]

        over(C, body)

    def coarse_down(C, D, r):
        w = C["w"]

        def body(x):
            total = None
            for half_ in range(2):
                centre, t = coarse_terms(C, r, 2 * x + half_)
                res = residue(centre, t, C["co"][0, 2 * x + half_], 0.25 ** C["l"])
                total = res if total is None else tuple(a + b for a, b in zip(total, res))
            for c in range(2):
                D["g"][c, x] = 0.125 * pair_sum(total[c], w, 4 * w)

        over(D, body)

    def coarse_up(C, D, r, rd):
        def body(x):
            for c in range(2):
                add = D["v"][rd, c, x + 1]
                for half_ in range(2):
                    C["v"][r, c, 2 * x + half_ + 1] = C["v"][r, c, 2 * x + half_ + 1] + add

        over(D, body)

    relax(fine, 0)
    arrive(fine, 1)
    side = sides(fine, 1)

    def down_plane(x, packed):
        a = residual(fine, 1, 2 * x, side)
        b = residual(fine, 1, 2 * x + 1, side)
        g = [0.125 * pair_sum(a[c] + b[c], 1, 1) for c in range(2)]
        for c in range(2):
            gl1[c, x] = g[c]
        return put(half, 0, x, first(co1[1, x], co1[2, x], g[0], g[1]), packed)

    packed = lax.fori_loop(0, X0 // 2, down_plane, jnp.zeros(tile, jnp.float32), unroll=True)
    seal(half, 0, packed)

    bulk(gm, 0).wait_recv()

    def store_mach(x, by, value):
        cc2[3, x, 4 * by:4 * by + 4, :] = value[:4]

    spread(gm, store_mach)
    over(coarse[0], lambda x: set_coefficients(cc2, x, cc2[3, x], 2))
    for C, D in zip(coarse[:-1], coarse[1:]):
        factor = 0.125 / (WAVE * 0.5 ** C["l"])

        def body(x, C=C, D=D, factor=factor):
            mach = factor * pair_sum(C["co"][3, 2 * x] + C["co"][3, 2 * x + 1], C["w"], 4 * C["w"])
            set_coefficients(D["co"], x, mach, D["l"])

        over(D, body)

    relax(half, 0)
    arrive(half, 1)
    side = sides(half, 1)
    groups = [jnp.zeros(tile, jnp.float32) for _ in range(2)]
    for x in range(XC):
        a = residual(half, 1, 2 * x, side)
        b = residual(half, 1, 2 * x + 1, side)
        for c in range(2):
            groups[c] = jnp.where(lane % 4 == x, 0.125 * pair_sum(a[c] + b[c], 2, 2), groups[c])
    for c in range(2):
        for y in range(4):
            gg[me, 4 * c + y:4 * c + y + 1, :] = groups[c][4 * y:4 * y + 1]
    tell(gg, 1)
    bulk(gm, 0).wait_send()
    bulk(gg, 1).wait_recv()

    def store_source(x, by, value):
        for c in range(2):
            gc2[c, x, 4 * by:4 * by + 4, :] = value[4 * c:4 * c + 4]

    spread(gg, store_source)

    for C, D in zip(coarse[:-1], coarse[1:]):
        coarse_first(C)
        coarse_relax(C, 0)
        coarse_down(C, D, 1)
    coarse_first(coarse[2])
    at = 0
    for _ in range(COARSE_SWEEPS - 1):
        coarse_relax(coarse[2], at)
        at = 1 - at
    for C, D in ((coarse[1], coarse[2]), (coarse[0], coarse[1])):
        coarse_up(C, D, 1, at)
        coarse_relax(C, 1)
        coarse_relax(C, 0)
        at = 1

    packed = jnp.zeros(tile, jnp.float32)
    for x in range(XC):
        for c in range(2):
            value = va[1, c, ix * XC + x + 1]
            only = jnp.where(clane % 4 == iz, value, 0.0)
            back = only + roll(only, 1, 1)
            back = back + roll(back, 2, 1)
            ahead = only + roll(only, LANES - 1, 1)
            ahead = ahead + roll(ahead, LANES - 2, 1)
            own[c, x] = jnp.where(clane % 4 <= iz, ahead, back)
    for x in range(XC):
        add = []
        for c in range(2):
            value = own[c, x, pl.ds(4 * iy, 1), :]
            full = jnp.broadcast_to(value, tile)
            for y in range(1, 4):
                value = own[c, x, pl.ds(4 * iy + y, 1), :]
                full = jnp.where(row >= 4 * y, value, full)
            add.append(full)
        for half_ in range(2):
            values = [v1[1, c, 2 * x + half_ + 1] + add[c] for c in range(2)]
            packed = put(half, 2, 2 * x + half_, values, packed)
    seal(half, 2, packed)
    bulk(gg, 1).wait_send()
    relax(half, 2)

    def store_half(x, values):
        for c in range(2):
            gl1[c, x] = values[c]

    last(half, 3, store_half)

    def up_plane(x, packed):
        values = [v0[1, c, x + 1] + gl1[c, x // 2] for c in range(2)]
        return put(fine, 2, x, values, packed)

    seal(fine, 2, lax.fori_loop(0, X0, up_plane, jnp.zeros(tile, jnp.float32), unroll=True))
    relax(fine, 2)

    def store_out(x, values):
        for c in range(2):
            out[c, x] = values[c]

    last(fine, 3, store_out)

    for earlier in flying:
        sent(*earlier)


def solution(mesh):
    sizes = tuple(mesh.shape[a] for a in AXES)
    nx, ny, nz = sizes
    count = nx * ny * nz

    def shards(source, mach):
        _, X, Y, Z = source.shape
        assert X == 16 and Y == 16 and Z == LANES and nz == 4, "unsupported sizes"
        f32 = jnp.float32
        yall = ny * Y // 4
        xs = [nx * X // 2**l for l in (2, 3, 4)]
        scratch = [
            pltpu.VMEM(source.shape, f32),
            pltpu.VMEM(mach.shape, mach.dtype),
            pltpu.SemaphoreType.DMA((2,)),
            pltpu.VMEM((4, 2, X + 2, Y, LANES), f32),
            pltpu.VMEM((4, 2, X // 2 + 2, Y, LANES), f32),
            pltpu.VMEM((2, X // 2, Y, LANES), f32),
            pltpu.VMEM((4, X, Y, LANES), f32),
            pltpu.VMEM((4, X // 2, Y, LANES), f32),
            pltpu.VMEM((4, 2, 2, X, LANES), f32),
            pltpu.VMEM((4, 2, 2, X, LANES), f32),
            pltpu.VMEM((4, 2, 2, X // 2, LANES), f32),
            pltpu.VMEM((4, 2, 2, X // 2, LANES), f32),
            pltpu.VMEM((8, Y, LANES), f32),
            pltpu.VMEM((8, 2, Y, LANES), f32),
            pltpu.VMEM((count, 8, LANES), f32),
            pltpu.VMEM((count, 8, LANES), f32),
        ]
        scratch += [pltpu.VMEM((2, 2, n + 2, yall, LANES), f32) for n in xs]
        scratch += [pltpu.VMEM((2, n, yall, LANES), f32) for n in xs]
        scratch += [pltpu.VMEM((4, n, yall, LANES), f32) for n in xs]
        scratch += [
            pltpu.VMEM((2, X // 4, yall, LANES), f32),
            pltpu.SemaphoreType.DMA((8, 6)),
            pltpu.SemaphoreType.DMA((8, 6)),
            pltpu.SemaphoreType.DMA((2,)),
            pltpu.SemaphoreType.DMA((2,)),
        ]
        return pl.pallas_call(
            functools.partial(kernel, sizes),
            out_shape=jax.ShapeDtypeStruct(source.shape, f32),
            in_specs=[pl.BlockSpec(memory_space=pl.ANY)] * 2,
            out_specs=pl.BlockSpec(memory_space=pltpu.VMEM),
            scratch_shapes=scratch,
            compiler_params=pltpu.CompilerParams(
                collective_id=0, has_side_effects=True, vmem_limit_bytes=48 * 2**20
            ),
        )(source, mach)

    return jax.shard_map(
        shards,
        mesh=mesh,
        in_specs=(P(None, "gx", "gy", "gz"), P("gx", "gy", "gz")),
        out_specs=P(None, "gx", "gy", "gz"),
        check_vma=False,
    )
```

```python
import functools

import jax
import jax.numpy as jnp
from jax import lax
from jax.experimental import pallas as pl
from jax.experimental.pallas import tpu as pltpu
from jax.sharding import PartitionSpec as P

MESH = pl.DeviceIdType.MESH
AXES = ("gx", "gy", "gz")
COARSE_SWEEPS = 6
WAVE = 0.25
WAVE2 = 0.0625
LANES = 128


def lane_of(shape):
    return lax.broadcasted_iota(jnp.int32, shape, len(shape) - 1)


def row_of(shape):
    return lax.broadcasted_iota(jnp.int32, shape, len(shape) - 2)


def roll(value, shift, axis):
    if isinstance(shift, int):
        shift %= value.shape[axis]
        if shift == 0:
            return value
    return pltpu.roll(value, shift, axis)


def turn(shift):
    return shift % LANES if isinstance(shift, int) else lax.rem(shift, LANES)


def coefficients(mach, level):
    scale = 0.25**level
    axial = scale * (1.0 - mach * mach)
    real = 2.0 * axial + (4.0 * scale - WAVE2)
    imaginary = 0.5 * WAVE2
    half = 0.5 / (real * real + imaginary * imaginary)
    return axial, real * half, -imaginary * half


def pair_sum(value, rows, lanes):
    shape = value.shape
    even = (row_of(shape) // rows) % 2 == 0
    value = value + jnp.where(even, roll(value, shape[0] - rows, 0), roll(value, rows, 0))
    even = (lane_of(shape) // lanes) % 2 == 0
    return value + jnp.where(even, roll(value, LANES - lanes, 1), roll(value, lanes, 1))


def kernel(sizes, g_hbm, mach_hbm, out, g0, mach_in, in_sem, tb, v0, v1, gl1, co0, co1, ys0, yr0, ys1, yr1, zs, zr, gm, gg,
           va, vb, vc, gc2, gc3, gc4, cc2, cc3, cc4, own, send_sem, recv_sem, gs_sem, gr_sem):
    nx, ny, nz = sizes
    count = nx * ny * nz
    ix, iy, iz = (lax.axis_index(a) for a in AXES)
    me = (ix * ny + iy) * nz + iz
    X0, Y0 = g0.shape[1], g0.shape[2]
    tile = (Y0, LANES)
    here = {"gx": ix, "gy": iy, "gz": iz}
    size = dict(zip(AXES, sizes))
    yall = va.shape[3]
    XC = X0 // 4

    def peer(d):
        t = lax.rem(me + d, count)
        return (t // (ny * nz), lax.rem(t // nz, ny), lax.rem(t, nz))

    loads = [
        pltpu.make_async_copy(mach_hbm, mach_in, in_sem.at[0]),
        pltpu.make_async_copy(g_hbm, g0, in_sem.at[1]),
    ]
    for load in loads:
        load.start()
    barrier = pltpu.get_barrier_semaphore()

    def greet(d, carry):
        pl.semaphore_signal(barrier, inc=1, device_id=peer(d), device_id_type=MESH)
        return carry

    for ref in (v0, v1):
        zero = jnp.zeros((2,) + tile, jnp.float32)
        for r in range(4):
            ref[r, :, 0] = zero
            ref[r, :, ref.shape[2] - 1] = zero
    yr0[...] = jnp.zeros(yr0.shape, jnp.float32)
    yr1[...] = jnp.zeros(yr1.shape, jnp.float32)
    zr[...] = jnp.zeros(zr.shape, jnp.float32)
    lax.fori_loop(1, count, greet, 0)

    lane, row = lane_of(tile), row_of(tile)
    levels = (
        dict(v=v0, g=g0, co=co0, ys=ys0, yr=yr0, X=X0, w=1, l=0),
        dict(v=v1, g=gl1, co=co1, ys=ys1, yr=yr1, X=X0 // 2, w=2, l=1),
    )

    def links(L, r):
        X, v, ys, yr = L["X"], L["v"].at[r], L["ys"].at[r], L["yr"].at[r]
        k = 4 * L["l"] + r
        pieces = []
        for n, (axis, step, src, dst) in enumerate((
            ("gz", 1, zs.at[k], zr.at[k, 0]),
            ("gz", -1, zs.at[k], zr.at[k, 1]),
            ("gy", 1, ys.at[1], yr.at[0]),
            ("gy", -1, ys.at[0], yr.at[1]),
            ("gx", 1, v.at[:, X], v.at[:, 0]),
            ("gx", -1, v.at[:, 1], v.at[:, X + 1]),
        )):
            at = here[axis]
            up, down = at < size[axis] - 1, at > 0
            to = tuple(here[a] + step if a == axis else here[a] for a in AXES)
            copy = pltpu.make_async_remote_copy(
                src_ref=src, dst_ref=dst, send_sem=send_sem.at[k, n], recv_sem=recv_sem.at[k, n],
                device_id=to, device_id_type=MESH,
            )
            pieces.append((copy, up if step > 0 else down, down if step > 0 else up, axis))
        return pieces

    def start(L, r, axes=AXES):
        for copy, sends, _, axis in links(L, r):
            if axis in axes:
                pl.when(sends)(copy.start)

    flying = []

    def arrive(L, r):
        for earlier in flying:
            sent(*earlier)
        flying[:] = [(L, r)]
        for copy, _, receives, _ in links(L, r):
            pl.when(receives)(copy.wait_recv)

    def sent(L, r):
        for copy, sends, _, _ in links(L, r):
            pl.when(sends)(copy.wait_send)

    def put(L, r, x, values, packed):
        v, ys = L["v"], L["ys"]
        for c in range(2):
            value = values[c]
            v[r, c, x + 1] = value
            ys[r, 0, c, pl.ds(x, 1), :] = value[:1]
            ys[r, 1, c, pl.ds(x, 1), :] = value[Y0 - 1:]
            packed = jnp.where(lane // 4 == x + 16 * c, roll(value, 4 * x + 2 + 64 * c, 1), packed)
        return packed

    def seal(L, r, packed, axes=AXES):
        zs[4 * L["l"] + r] = packed
        start(L, r, axes)

    def sides(L, r):
        k, w = 4 * L["l"] + r, L["w"]
        below = (lane % 4 >= 2 - w) & (lane % 4 < 2)
        return jnp.where(below, zr[k, 0], roll(zr[k, 1], LANES - 2 * w, 1))

    def inside(L, r):
        v, w, co, g, X = L["v"], L["w"], L["co"], L["g"], L["X"]
        scale = 0.25 ** L["l"]

        def plane(x, west=True, east=True):
            axial, drift = co[0, x], co[3, x]
            t = []
            for c in range(2):
                value = v[r, c, x + 1]
                lower = jnp.where(lane < w, 0.0, roll(value, w, 1))
                upper = jnp.where(lane >= LANES - w, 0.0, roll(value, LANES - w, 1))
                south = jnp.where(row < w, 0.0, roll(value, w, 0))
                north = jnp.where(row >= Y0 - w, 0.0, roll(value, Y0 - w, 0))
                t.append(g[c, x] + scale * ((lower + upper) + (south + north)))
            e = [v[r, c, x + 2] for c in range(2)] if east else None
            o = [v[r, c, x] for c in range(2)] if west else None
            if east and west:
                along = [e[c] + o[c] for c in range(2)]
                slope = [e[c] - o[c] for c in range(2)]
            elif east:
                along, slope = e, e
            else:
                along, slope = o, [-o[0], -o[1]]
            tb[0, x] = t[0] + axial * along[0] - drift * slope[1]
            tb[1, x] = t[1] + axial * along[1] + drift * slope[0]

        def middle(x, carry):
            plane(x)
            return carry

        plane(0, west=False)
        plane(X - 1, east=False)
        lax.fori_loop(1, X - 1, middle, 0, unroll=True)

    def terms(L, r, x, side):
        v, yr, w, X, co = L["v"], L["yr"], L["w"], L["X"], L["co"]
        scale = 0.25 ** L["l"]
        rim = (lane < w) | (lane >= LANES - w)
        t = []
        for c in range(2):
            shift = turn(4 * LANES - (4 * x + 2 - w + 64 * c))
            add = jnp.where(rim, roll(side, shift, 1), 0.0)
            south = jnp.where(row < w, yr[r, 0, c, pl.ds(x, 1), :], 0.0)
            add = add + jnp.where(row >= Y0 - w, yr[r, 1, c, pl.ds(x, 1), :], south)
            t.append(tb[c, x] + (scale * add if L["l"] else add))
        if isinstance(x, int) and x in (0, X - 1):
            axial, drift = co[0, x], co[3, x]
            e = [v[r, c, 0 if x == 0 else X + 1] for c in range(2)]
            if x == 0:
                drift = -drift
            t = [t[0] + axial * e[0] - drift * e[1], t[1] + axial * e[1] + drift * e[0]]
        return [v[r, c, x + 1] for c in range(2)], t

    def relaxed(centre, t, hr, hi):
        return (0.5 * centre[0] + (hr * t[0] - hi * t[1]), 0.5 * centre[1] + (hi * t[0] + hr * t[1]))

    def residue(centre, t, axial, scale):
        dr = 2.0 * axial + (4.0 * scale - WAVE2)
        di = 0.5 * WAVE2
        return (t[0] - dr * centre[0] + di * centre[1], t[1] - dr * centre[1] - di * centre[0])

    def relax(L, r):
        inside(L, r)
        arrive(L, r)
        side = sides(L, r)
        co, X = L["co"], L["X"]

        def body(x, packed):
            centre, t = terms(L, r, x, side)
            return put(L, r + 1, x, relaxed(centre, t, co[1, x], co[2, x]), packed)

        packed = body(X - 1, body(0, jnp.zeros(tile, jnp.float32)))
        start(L, r + 1, "gx")
        seal(L, r + 1, lax.fori_loop(1, X - 1, body, packed, unroll=True), ("gy", "gz"))

    def last(L, r, store):
        inside(L, r)
        arrive(L, r)
        side = sides(L, r)
        co, X = L["co"], L["X"]

        def body(x, carry):
            centre, t = terms(L, r, x, side)
            store(x, relaxed(centre, t, co[1, x], co[2, x]))
            return carry

        body(X - 1, body(0, 0))
        lax.fori_loop(1, X - 1, body, 0, unroll=True)

    def residual(L, r, x, side):
        centre, t = terms(L, r, x, side)
        return residue(centre, t, L["co"][0, x], 0.25 ** L["l"])

    def set_coefficients(co, x, mach, level):
        axial, hr, hi = coefficients(mach, level)
        co[0, x] = axial
        co[1, x] = hr
        co[2, x] = hi
        co[3, x] = (WAVE * 0.5**level) * mach
        return hr, hi

    def first(hr, hi, gr, gi):
        return hr * gr - hi * gi, hr * gi + hi * gr

    fine, half = levels

    def open_plane(x, packed):
        mach = mach_in[x].astype(jnp.float32)
        hr, hi = set_coefficients(co0, x, mach, 0)
        return put(fine, 0, x, first(hr, hi, g0[0, x], g0[1, x]), packed)

    for load in loads:
        load.wait()
    packed = lax.fori_loop(0, X0, open_plane, jnp.zeros(tile, jnp.float32), unroll=True)

    def mach_plane(x, carry):
        mach = mach_in[2 * x].astype(jnp.float32) + mach_in[2 * x + 1].astype(jnp.float32)
        set_coefficients(co1, x, 0.125 * pair_sum(mach, 1, 1), 1)
        return carry

    pl.semaphore_wait(barrier, count - 1)
    seal(fine, 0, packed)

    lax.fori_loop(0, X0 // 2, mach_plane, 0, unroll=True)
    undo = 1.0 / (WAVE * 0.5)
    group = jnp.zeros(tile, jnp.float32)
    for x in range(XC):
        mach = pair_sum((co1[3, 2 * x] + co1[3, 2 * x + 1]) * undo, 2, 2) * 0.125
        group = jnp.where(lane % 4 == x, mach, group)
    for y in range(4):
        gm[me, y:y + 1, :] = group[4 * y:4 * y + 1]
        gm[me, y + 4:y + 5, :] = group[4 * y:4 * y + 1]

    def tell(ref, n):
        def one(d, carry):
            pltpu.make_async_remote_copy(
                src_ref=ref.at[me], dst_ref=ref.at[me], send_sem=gs_sem.at[n], recv_sem=gr_sem.at[n],
                device_id=peer(d), device_id_type=MESH,
            ).start()
            return carry

        lax.fori_loop(1, count, one, 0)

    def bulk(ref, n):
        part = ref.at[pl.ds(0, count - 1)]
        return pltpu.make_async_remote_copy(
            src_ref=part, dst_ref=part, send_sem=gs_sem.at[n], recv_sem=gr_sem.at[n],
            device_id=peer(1), device_id_type=MESH,
        )

    def spread(ref, store):
        lane8 = lane_of((8, LANES))

        def block(bx, carry):
            for by in range(ny):
                tiles = [ref[(bx * ny + by) * nz + bz] for bz in range(nz)]
                for x in range(XC):
                    value = tiles[0]
                    for bz in range(nz):
                        moved = roll(tiles[bz], bz - x, 1)
                        value = moved if bz == 0 else jnp.where(lane8 % 4 == bz, moved, value)
                    store(bx * XC + x, by, value)
            return carry

        lax.fori_loop(0, nx, block, 0, unroll=True if nx <= 4 else 1)

    tell(gm, 0)

    wide = (yall, LANES)
    clane, crow = lane_of(wide), row_of(wide)
    coarse = (
        dict(v=va, g=gc2, co=cc2, w=1, l=2),
        dict(v=vb, g=gc3, co=cc3, w=2, l=3),
        dict(v=vc, g=gc4, co=cc4, w=4, l=4),
    )
    for C in coarse:
        v = C["v"]
        C["X"] = v.shape[2] - 2
        C["unroll"] = True if C["X"] <= 16 else 4
        for r in range(2):
            for c in range(2):
                v[r, c, 0] = jnp.zeros(wide, jnp.float32)
                v[r, c, C["X"] + 1] = jnp.zeros(wide, jnp.float32)

    def over(C, body):
        def step(x, carry):
            body(x)
            return carry

        lax.fori_loop(0, C["X"], step, 0, unroll=C["unroll"])

    def coarse_terms(C, r, x):
        v, w, co, g = C["v"], C["w"], C["co"], C["g"]
        m = 4 * w
        scale = 0.25 ** C["l"]
        top = clane >= LANES - m
        centre, along, across, slope = [], [], [], []
        for c in range(2):
            value = v[r, c, x + 1]
            east, west = v[r, c, x + 2], v[r, c, x]
            upper = jnp.where(top, roll(value, LANES - m - 1, 1), roll(value, LANES - m, 1))
            upper = jnp.where(top & (clane % 4 == 3), 0.0, upper)
            lower = jnp.where(clane < m, roll(value, m + 1, 1), roll(value, m, 1))
            lower = jnp.where((clane < m) & (clane % 4 == 0), 0.0, lower)
            south = jnp.where(crow < w, 0.0, roll(value, w, 0))
            north = jnp.where(crow >= yall - w, 0.0, roll(value, yall - w, 0))
            centre.append(value)
            across.append(scale * ((lower + upper) + (south + north)))
            along.append(east + west)
            slope.append(east - west)
        real = g[0, x] + co[0, x] * along[0] + across[0] - co[3, x] * slope[1]
        imaginary = g[1, x] + co[0, x] * along[1] + across[1] + co[3, x] * slope[0]
        return centre, (real, imaginary)

    def coarse_first(C):
        def body(x):
            g, co = C["g"], C["co"]
            values = first(co[1, x], co[2, x], g[0, x], g[1, x])
            for c in range(2):
                C["v"][0, c, x + 1] = values[c]

        over(C, body)

    def coarse_relax(C, r):
        def body(x):
            centre, t = coarse_terms(C, r, x)
            values = relaxed(centre, t, C["co"][1, x], C["co"][2, x])
            for c in range(2):
                C["v"][1 - r, c, x + 1] = values[c]

        over(C, body)

    def coarse_down(C, D, r):
        w = C["w"]

        def body(x):
            total = None
            for half_ in range(2):
                centre, t = coarse_terms(C, r, 2 * x + half_)
                res = residue(centre, t, C["co"][0, 2 * x + half_], 0.25 ** C["l"])
                total = res if total is None else tuple(a + b for a, b in zip(total, res))
            for c in range(2):
                D["g"][c, x] = 0.125 * pair_sum(total[c], w, 4 * w)

        over(D, body)

    def coarse_up(C, D, r, rd):
        def body(x):
            for c in range(2):
                add = D["v"][rd, c, x + 1]
                for half_ in range(2):
                    C["v"][r, c, 2 * x + half_ + 1] = C["v"][r, c, 2 * x + half_ + 1] + add

        over(D, body)

    relax(fine, 0)
    inside(fine, 1)
    arrive(fine, 1)
    side = sides(fine, 1)

    def down_plane(x, packed):
        a = residual(fine, 1, 2 * x, side)
        b = residual(fine, 1, 2 * x + 1, side)
        g = [0.125 * pair_sum(a[c] + b[c], 1, 1) for c in range(2)]
        for c in range(2):
            gl1[c, x] = g[c]
        return put(half, 0, x, first(co1[1, x], co1[2, x], g[0], g[1]), packed)

    packed = down_plane(X0 // 2 - 1, down_plane(0, jnp.zeros(tile, jnp.float32)))
    start(half, 0, "gx")
    packed = lax.fori_loop(1, X0 // 2 - 1, down_plane, packed, unroll=True)
    seal(half, 0, packed, ("gy", "gz"))

    bulk(gm, 0).wait_recv()

    def store_mach(x, by, value):
        cc2[3, x, 4 * by:4 * by + 4, :] = value[:4]

    spread(gm, store_mach)
    over(coarse[0], lambda x: set_coefficients(cc2, x, cc2[3, x], 2))
    for C, D in zip(coarse[:-1], coarse[1:]):
        factor = 0.125 / (WAVE * 0.5 ** C["l"])

        def body(x, C=C, D=D, factor=factor):
            mach = factor * pair_sum(C["co"][3, 2 * x] + C["co"][3, 2 * x + 1], C["w"], 4 * C["w"])
            set_coefficients(D["co"], x, mach, D["l"])

        over(D, body)

    relax(half, 0)
    inside(half, 1)
    arrive(half, 1)
    side = sides(half, 1)
    groups = [jnp.zeros(tile, jnp.float32) for _ in range(2)]
    for x in range(XC):
        a = residual(half, 1, 2 * x, side)
        b = residual(half, 1, 2 * x + 1, side)
        for c in range(2):
            groups[c] = jnp.where(lane % 4 == x, 0.125 * pair_sum(a[c] + b[c], 2, 2), groups[c])
    for c in range(2):
        for y in range(4):
            gg[me, 4 * c + y:4 * c + y + 1, :] = groups[c][4 * y:4 * y + 1]
    tell(gg, 1)
    bulk(gm, 0).wait_send()
    bulk(gg, 1).wait_recv()

    def store_source(x, by, value):
        for c in range(2):
            gc2[c, x, 4 * by:4 * by + 4, :] = value[4 * c:4 * c + 4]

    spread(gg, store_source)

    for C, D in zip(coarse[:-1], coarse[1:]):
        coarse_first(C)
        coarse_relax(C, 0)
        coarse_down(C, D, 1)
    coarse_first(coarse[2])
    at = 0
    for _ in range(COARSE_SWEEPS - 1):
        coarse_relax(coarse[2], at)
        at = 1 - at
    for C, D in ((coarse[1], coarse[2]), (coarse[0], coarse[1])):
        coarse_up(C, D, 1, at)
        coarse_relax(C, 1)
        coarse_relax(C, 0)
        at = 1

    packed = jnp.zeros(tile, jnp.float32)
    for x in range(XC):
        for c in range(2):
            value = va[1, c, ix * XC + x + 1]
            only = jnp.where(clane % 4 == iz, value, 0.0)
            back = only + roll(only, 1, 1)
            back = back + roll(back, 2, 1)
            ahead = only + roll(only, LANES - 1, 1)
            ahead = ahead + roll(ahead, LANES - 2, 1)
            own[c, x] = jnp.where(clane % 4 <= iz, ahead, back)
    for x in range(XC):
        add = []
        for c in range(2):
            value = own[c, x, pl.ds(4 * iy, 1), :]
            full = jnp.broadcast_to(value, tile)
            for y in range(1, 4):
                value = own[c, x, pl.ds(4 * iy + y, 1), :]
                full = jnp.where(row >= 4 * y, value, full)
            add.append(full)
        for half_ in range(2):
            values = [v1[1, c, 2 * x + half_ + 1] + add[c] for c in range(2)]
            packed = put(half, 2, 2 * x + half_, values, packed)
    seal(half, 2, packed)
    bulk(gg, 1).wait_send()
    relax(half, 2)

    def store_half(x, values):
        for c in range(2):
            gl1[c, x] = values[c]

    last(half, 3, store_half)

    def up_plane(x, packed):
        values = [v0[1, c, x + 1] + gl1[c, x // 2] for c in range(2)]
        return put(fine, 2, x, values, packed)

    seal(fine, 2, lax.fori_loop(0, X0, up_plane, jnp.zeros(tile, jnp.float32), unroll=True))
    relax(fine, 2)

    def store_out(x, values):
        for c in range(2):
            out[c, x] = values[c]

    last(fine, 3, store_out)

    for earlier in flying:
        sent(*earlier)


def solution(mesh):
    sizes = tuple(mesh.shape[a] for a in AXES)
    nx, ny, nz = sizes
    count = nx * ny * nz

    def shards(source, mach):
        _, X, Y, Z = source.shape
        assert X == 16 and Y == 16 and Z == LANES and nz == 4, "unsupported sizes"
        f32 = jnp.float32
        yall = ny * Y // 4
        xs = [nx * X // 2**l for l in (2, 3, 4)]
        scratch = [
            pltpu.VMEM(source.shape, f32),
            pltpu.VMEM(mach.shape, mach.dtype),
            pltpu.SemaphoreType.DMA((2,)),
            pltpu.VMEM((2, X, Y, LANES), f32),
            pltpu.VMEM((4, 2, X + 2, Y, LANES), f32),
            pltpu.VMEM((4, 2, X // 2 + 2, Y, LANES), f32),
            pltpu.VMEM((2, X // 2, Y, LANES), f32),
            pltpu.VMEM((4, X, Y, LANES), f32),
            pltpu.VMEM((4, X // 2, Y, LANES), f32),
            pltpu.VMEM((4, 2, 2, X, LANES), f32),
            pltpu.VMEM((4, 2, 2, X, LANES), f32),
            pltpu.VMEM((4, 2, 2, X // 2, LANES), f32),
            pltpu.VMEM((4, 2, 2, X // 2, LANES), f32),
            pltpu.VMEM((8, Y, LANES), f32),
            pltpu.VMEM((8, 2, Y, LANES), f32),
            pltpu.VMEM((count, 8, LANES), f32),
            pltpu.VMEM((count, 8, LANES), f32),
        ]
        scratch += [pltpu.VMEM((2, 2, n + 2, yall, LANES), f32) for n in xs]
        scratch += [pltpu.VMEM((2, n, yall, LANES), f32) for n in xs]
        scratch += [pltpu.VMEM((4, n, yall, LANES), f32) for n in xs]
        scratch += [
            pltpu.VMEM((2, X // 4, yall, LANES), f32),
            pltpu.SemaphoreType.DMA((8, 6)),
            pltpu.SemaphoreType.DMA((8, 6)),
            pltpu.SemaphoreType.DMA((2,)),
            pltpu.SemaphoreType.DMA((2,)),
        ]
        return pl.pallas_call(
            functools.partial(kernel, sizes),
            out_shape=jax.ShapeDtypeStruct(source.shape, f32),
            in_specs=[pl.BlockSpec(memory_space=pltpu.HBM)] * 2,
            out_specs=pl.BlockSpec(memory_space=pltpu.VMEM),
            scratch_shapes=scratch,
            compiler_params=pltpu.CompilerParams(
                collective_id=0, has_side_effects=True, vmem_limit_bytes=48 * 2**20
            ),
        )(source, mach)

    return jax.shard_map(
        shards,
        mesh=mesh,
        in_specs=(P(None, "gx", "gy", "gz"), P("gx", "gy", "gz")),
        out_specs=P(None, "gx", "gy", "gz"),
        check_vma=False,
    )
```

```python
import functools

import jax
import jax.numpy as jnp
from jax import lax
from jax.experimental import pallas as pl
from jax.experimental.pallas import tpu as pltpu
from jax.sharding import PartitionSpec as P

MESH = pl.DeviceIdType.MESH
AXES = ("gx", "gy", "gz")
COARSE_SWEEPS = 6
WAVE = 0.25
WAVE2 = 0.0625
LANES = 128


def lane_of(shape):
    return lax.broadcasted_iota(jnp.int32, shape, len(shape) - 1)


def row_of(shape):
    return lax.broadcasted_iota(jnp.int32, shape, len(shape) - 2)


def roll(value, shift, axis):
    if isinstance(shift, int):
        shift %= value.shape[axis]
        if shift == 0:
            return value
    return pltpu.roll(value, shift, axis)


def coefficients(mach, level):
    scale = 0.25**level
    axial = scale * (1.0 - mach * mach)
    real = 2.0 * axial + (4.0 * scale - WAVE2)
    imaginary = 0.5 * WAVE2
    half = 0.5 / (real * real + imaginary * imaginary)
    return axial, real * half, -imaginary * half


def pair_sum(value, rows, lanes):
    shape = value.shape
    even = (row_of(shape) // rows) % 2 == 0
    value = value + jnp.where(even, roll(value, shape[0] - rows, 0), roll(value, rows, 0))
    even = (lane_of(shape) // lanes) % 2 == 0
    return value + jnp.where(even, roll(value, LANES - lanes, 1), roll(value, lanes, 1))


def kernel(sizes, g_hbm, mach_hbm, out, g0, mach_in, in_sem, v0, v1, gl1, co0, co1, ys0, yr0, ys1, yr1, zs, zr, gm, gg,
           va, vb, vc, gc2, gc3, gc4, cc2, cc3, cc4, own, send_sem, recv_sem, gs_sem, gr_sem):
    nx, ny, nz = sizes
    count = nx * ny * nz
    ix, iy, iz = (lax.axis_index(a) for a in AXES)
    me = (ix * ny + iy) * nz + iz
    X0, Y0 = g0.shape[1], g0.shape[2]
    tile = (Y0, LANES)
    here = {"gx": ix, "gy": iy, "gz": iz}
    size = dict(zip(AXES, sizes))
    yall = va.shape[3]
    XC = X0 // 4

    def peer(d):
        t = lax.rem(me + d, count)
        return (t // (ny * nz), lax.rem(t // nz, ny), lax.rem(t, nz))

    around = [[lax.rem(i + d, n) for d in range(n)] for i, n in zip((ix, iy, iz), sizes)]

    def each_peer(act):
        if count > 64:
            def one(d, carry):
                act(peer(d))
                return carry

            lax.fori_loop(1, count, one, 0)
            return
        for c in range(nz):
            for a in range(nx):
                for b in range(ny):
                    if a or b or c:
                        act((around[0][a], around[1][b], around[2][c]))

    loads = [
        pltpu.make_async_copy(mach_hbm, mach_in, in_sem.at[0]),
        pltpu.make_async_copy(g_hbm, g0, in_sem.at[1]),
    ]
    for load in loads:
        load.start()
    barrier = pltpu.get_barrier_semaphore()

    def greet(to):
        pl.semaphore_signal(barrier, inc=1, device_id=to, device_id_type=MESH)

    for ref in (v0, v1):
        zero = jnp.zeros((2,) + tile, jnp.float32)
        for r in range(4):
            ref[r, :, 0] = zero
            ref[r, :, ref.shape[2] - 1] = zero
    yr0[...] = jnp.zeros(yr0.shape, jnp.float32)
    yr1[...] = jnp.zeros(yr1.shape, jnp.float32)
    zr[...] = jnp.zeros(zr.shape, jnp.float32)
    each_peer(greet)

    lane, row = lane_of(tile), row_of(tile)
    levels = (
        dict(v=v0, g=g0, co=co0, ys=ys0, yr=yr0, X=X0, w=1, l=0),
        dict(v=v1, g=gl1, co=co1, ys=ys1, yr=yr1, X=X0 // 2, w=2, l=1),
    )

    def links(L, r):
        X, v, ys, yr = L["X"], L["v"].at[r], L["ys"].at[r], L["yr"].at[r]
        k = 4 * L["l"] + r
        pieces = []
        for n, (axis, step, src, dst) in enumerate((
            ("gz", 1, zs.at[k], zr.at[k, 0]),
            ("gz", -1, zs.at[k], zr.at[k, 1]),
            ("gy", 1, ys.at[1], yr.at[0]),
            ("gy", -1, ys.at[0], yr.at[1]),
            ("gx", 1, v.at[:, X], v.at[:, 0]),
            ("gx", -1, v.at[:, 1], v.at[:, X + 1]),
        )):
            at = here[axis]
            up, down = at < size[axis] - 1, at > 0
            to = tuple(here[a] + step if a == axis else here[a] for a in AXES)
            copy = pltpu.make_async_remote_copy(
                src_ref=src, dst_ref=dst, send_sem=send_sem.at[k, n], recv_sem=recv_sem.at[k, n],
                device_id=to, device_id_type=MESH,
            )
            pieces.append((copy, up if step > 0 else down, down if step > 0 else up))
        return pieces

    def start(L, r):
        for copy, sends, _ in links(L, r):
            pl.when(sends)(copy.start)

    flying = []

    def arrive(L, r):
        for earlier in flying:
            sent(*earlier)
        flying[:] = [(L, r)]
        for copy, _, receives in links(L, r):
            pl.when(receives)(copy.wait_recv)

    def sent(L, r):
        for copy, sends, _ in links(L, r):
            pl.when(sends)(copy.wait_send)

    def put(L, r, x, values, packed):
        v, ys = L["v"], L["ys"]
        for c in range(2):
            value = values[c]
            v[r, c, x + 1] = value
            ys[r, 0, c, pl.ds(x, 1), :] = value[:1]
            ys[r, 1, c, pl.ds(x, 1), :] = value[Y0 - 1:]
            packed = jnp.where(lane // 4 == x + 16 * c, roll(value, 4 * x + 2 + 64 * c, 1), packed)
        return packed

    def seal(L, r, packed):
        zs[4 * L["l"] + r] = packed
        start(L, r)

    def sides(L, r):
        k, w = 4 * L["l"] + r, L["w"]
        below = (lane % 4 >= 2 - w) & (lane % 4 < 2)
        return jnp.where(below, zr[k, 0], roll(zr[k, 1], LANES - 2 * w, 1))

    def terms(L, r, x, side):
        v, yr, w, co = L["v"], L["yr"], L["w"], L["co"]
        scale = 0.25 ** L["l"]
        axial, drift = co[0, x], co[3, x]
        centre, along, across = [], [], []
        slope = []
        for c in range(2):
            here_ = v[r, c, x + 1]
            east, west = v[r, c, x + 2], v[r, c, x]
            shift = lax.rem(4 * LANES - (4 * x + 2 - w + 64 * c), LANES)
            edge = roll(side, shift, 1)
            lower = jnp.where(lane < w, edge, roll(here_, w, 1))
            upper = jnp.where(lane >= LANES - w, edge, roll(here_, LANES - w, 1))
            south = jnp.where(row < w, yr[r, 0, c, pl.ds(x, 1), :], roll(here_, w, 0))
            north = jnp.where(row >= Y0 - w, yr[r, 1, c, pl.ds(x, 1), :], roll(here_, Y0 - w, 0))
            centre.append(here_)
            across.append((lower + upper) + (south + north))
            along.append(east + west)
            slope.append(east - west)
        if L["l"]:
            across = [scale * a for a in across]
        g = L["g"]
        real = g[0, x] + axial * along[0] + across[0] - drift * slope[1]
        imaginary = g[1, x] + axial * along[1] + across[1] + drift * slope[0]
        return centre, (real, imaginary)

    def relaxed(centre, t, hr, hi):
        return (0.5 * centre[0] + (hr * t[0] - hi * t[1]), 0.5 * centre[1] + (hi * t[0] + hr * t[1]))

    def residue(centre, t, axial, scale):
        dr = 2.0 * axial + (4.0 * scale - WAVE2)
        di = 0.5 * WAVE2
        return (t[0] - dr * centre[0] + di * centre[1], t[1] - dr * centre[1] - di * centre[0])

    def relax(L, r):
        arrive(L, r)
        side = sides(L, r)
        co = L["co"]

        def body(x, packed):
            centre, t = terms(L, r, x, side)
            return put(L, r + 1, x, relaxed(centre, t, co[1, x], co[2, x]), packed)

        seal(L, r + 1, lax.fori_loop(0, L["X"], body, jnp.zeros(tile, jnp.float32), unroll=True))

    def last(L, r, store):
        arrive(L, r)
        side = sides(L, r)
        co = L["co"]

        def body(x, carry):
            centre, t = terms(L, r, x, side)
            store(x, relaxed(centre, t, co[1, x], co[2, x]))
            return carry

        lax.fori_loop(0, L["X"], body, 0, unroll=True)

    def residual(L, r, x, side):
        centre, t = terms(L, r, x, side)
        return residue(centre, t, L["co"][0, x], 0.25 ** L["l"])

    def set_coefficients(co, x, mach, level):
        axial, hr, hi = coefficients(mach, level)
        co[0, x] = axial
        co[1, x] = hr
        co[2, x] = hi
        co[3, x] = (WAVE * 0.5**level) * mach
        return hr, hi

    def first(hr, hi, gr, gi):
        return hr * gr - hi * gi, hr * gi + hi * gr

    fine, half = levels

    def open_plane(x, packed):
        mach = mach_in[x].astype(jnp.float32)
        hr, hi = set_coefficients(co0, x, mach, 0)
        return put(fine, 0, x, first(hr, hi, g0[0, x], g0[1, x]), packed)

    for load in loads:
        load.wait()
    packed = lax.fori_loop(0, X0, open_plane, jnp.zeros(tile, jnp.float32), unroll=True)

    def mach_plane(x, carry):
        mach = mach_in[2 * x].astype(jnp.float32) + mach_in[2 * x + 1].astype(jnp.float32)
        set_coefficients(co1, x, 0.125 * pair_sum(mach, 1, 1), 1)
        return carry

    pl.semaphore_wait(barrier, count - 1)
    seal(fine, 0, packed)

    lax.fori_loop(0, X0 // 2, mach_plane, 0, unroll=True)
    undo = 1.0 / (WAVE * 0.5)
    group = jnp.zeros(tile, jnp.float32)
    for x in range(XC):
        mach = pair_sum((co1[3, 2 * x] + co1[3, 2 * x + 1]) * undo, 2, 2) * 0.125
        group = jnp.where(lane % 4 == x, mach, group)
    for y in range(4):
        gm[me, y:y + 1, :] = group[4 * y:4 * y + 1]
        gm[me, y + 4:y + 5, :] = group[4 * y:4 * y + 1]

    def tell(ref, n):
        def one(to):
            pltpu.make_async_remote_copy(
                src_ref=ref.at[me], dst_ref=ref.at[me], send_sem=gs_sem.at[n], recv_sem=gr_sem.at[n],
                device_id=to, device_id_type=MESH,
            ).start()

        each_peer(one)

    def bulk(ref, n):
        part = ref.at[pl.ds(0, count - 1)]
        return pltpu.make_async_remote_copy(
            src_ref=part, dst_ref=part, send_sem=gs_sem.at[n], recv_sem=gr_sem.at[n],
            device_id=(around[0][1], iy, iz), device_id_type=MESH,
        )

    def spread(ref, store):
        lane8 = lane_of((8, LANES))

        def block(bx, carry):
            for by in range(ny):
                tiles = [ref[(bx * ny + by) * nz + bz] for bz in range(nz)]
                for x in range(XC):
                    value = tiles[0]
                    for bz in range(nz):
                        moved = roll(tiles[bz], bz - x, 1)
                        value = moved if bz == 0 else jnp.where(lane8 % 4 == bz, moved, value)
                    store(bx * XC + x, by, value)
            return carry

        lax.fori_loop(0, nx, block, 0, unroll=True if nx <= 4 else 1)

    tell(gm, 0)

    wide = (yall, LANES)
    clane, crow = lane_of(wide), row_of(wide)
    coarse = (
        dict(v=va, g=gc2, co=cc2, w=1, l=2),
        dict(v=vb, g=gc3, co=cc3, w=2, l=3),
        dict(v=vc, g=gc4, co=cc4, w=4, l=4),
    )
    for C in coarse:
        v = C["v"]
        C["X"] = v.shape[2] - 2
        C["unroll"] = True if C["X"] <= 16 else 4
        for r in range(2):
            for c in range(2):
                v[r, c, 0] = jnp.zeros(wide, jnp.float32)
                v[r, c, C["X"] + 1] = jnp.zeros(wide, jnp.float32)

    def over(C, body):
        def step(x, carry):
            body(x)
            return carry

        lax.fori_loop(0, C["X"], step, 0, unroll=C["unroll"])

    def coarse_terms(C, r, x):
        v, w, co, g = C["v"], C["w"], C["co"], C["g"]
        m = 4 * w
        scale = 0.25 ** C["l"]
        top = clane >= LANES - m
        centre, along, across, slope = [], [], [], []
        for c in range(2):
            value = v[r, c, x + 1]
            east, west = v[r, c, x + 2], v[r, c, x]
            upper = jnp.where(top, roll(value, LANES - m - 1, 1), roll(value, LANES - m, 1))
            upper = jnp.where(top & (clane % 4 == 3), 0.0, upper)
            lower = jnp.where(clane < m, roll(value, m + 1, 1), roll(value, m, 1))
            lower = jnp.where((clane < m) & (clane % 4 == 0), 0.0, lower)
            south = jnp.where(crow < w, 0.0, roll(value, w, 0))
            north = jnp.where(crow >= yall - w, 0.0, roll(value, yall - w, 0))
            centre.append(value)
            across.append(scale * ((lower + upper) + (south + north)))
            along.append(east + west)
            slope.append(east - west)
        real = g[0, x] + co[0, x] * along[0] + across[0] - co[3, x] * slope[1]
        imaginary = g[1, x] + co[0, x] * along[1] + across[1] + co[3, x] * slope[0]
        return centre, (real, imaginary)

    def coarse_first(C):
        def body(x):
            g, co = C["g"], C["co"]
            values = first(co[1, x], co[2, x], g[0, x], g[1, x])
            for c in range(2):
                C["v"][0, c, x + 1] = values[c]

        over(C, body)

    def coarse_relax(C, r):
        def body(x):
            centre, t = coarse_terms(C, r, x)
            values = relaxed(centre, t, C["co"][1, x], C["co"][2, x])
            for c in range(2):
                C["v"][1 - r, c, x + 1] = values[c]

        over(C, body)

    def coarse_down(C, D, r):
        w = C["w"]

        def body(x):
            total = None
            for half_ in range(2):
                centre, t = coarse_terms(C, r, 2 * x + half_)
                res = residue(centre, t, C["co"][0, 2 * x + half_], 0.25 ** C["l"])
                total = res if total is None else tuple(a + b for a, b in zip(total, res))
            for c in range(2):
                D["g"][c, x] = 0.125 * pair_sum(total[c], w, 4 * w)

        over(D, body)

    def coarse_up(C, D, r, rd):
        def body(x):
            for c in range(2):
                add = D["v"][rd, c, x + 1]
                for half_ in range(2):
                    C["v"][r, c, 2 * x + half_ + 1] = C["v"][r, c, 2 * x + half_ + 1] + add

        over(D, body)

    relax(fine, 0)
    arrive(fine, 1)
    side = sides(fine, 1)

    def down_plane(x, packed):
        a = residual(fine, 1, 2 * x, side)
        b = residual(fine, 1, 2 * x + 1, side)
        g = [0.125 * pair_sum(a[c] + b[c], 1, 1) for c in range(2)]
        for c in range(2):
            gl1[c, x] = g[c]
        return put(half, 0, x, first(co1[1, x], co1[2, x], g[0], g[1]), packed)

    packed = lax.fori_loop(0, X0 // 2, down_plane, jnp.zeros(tile, jnp.float32), unroll=True)
    seal(half, 0, packed)

    bulk(gm, 0).wait_recv()

    def store_mach(x, by, value):
        cc2[3, x, 4 * by:4 * by + 4, :] = value[:4]

    spread(gm, store_mach)
    over(coarse[0], lambda x: set_coefficients(cc2, x, cc2[3, x], 2))
    for C, D in zip(coarse[:-1], coarse[1:]):
        factor = 0.125 / (WAVE * 0.5 ** C["l"])

        def body(x, C=C, D=D, factor=factor):
            mach = factor * pair_sum(C["co"][3, 2 * x] + C["co"][3, 2 * x + 1], C["w"], 4 * C["w"])
            set_coefficients(D["co"], x, mach, D["l"])

        over(D, body)

    relax(half, 0)
    arrive(half, 1)
    side = sides(half, 1)
    groups = [jnp.zeros(tile, jnp.float32) for _ in range(2)]
    for x in range(XC):
        a = residual(half, 1, 2 * x, side)
        b = residual(half, 1, 2 * x + 1, side)
        for c in range(2):
            groups[c] = jnp.where(lane % 4 == x, 0.125 * pair_sum(a[c] + b[c], 2, 2), groups[c])
    for c in range(2):
        for y in range(4):
            gg[me, 4 * c + y:4 * c + y + 1, :] = groups[c][4 * y:4 * y + 1]
    tell(gg, 1)
    bulk(gm, 0).wait_send()
    bulk(gg, 1).wait_recv()

    def store_source(x, by, value):
        for c in range(2):
            gc2[c, x, 4 * by:4 * by + 4, :] = value[4 * c:4 * c + 4]

    spread(gg, store_source)

    for C, D in zip(coarse[:-1], coarse[1:]):
        coarse_first(C)
        coarse_relax(C, 0)
        coarse_down(C, D, 1)
    coarse_first(coarse[2])
    at = 0
    for _ in range(COARSE_SWEEPS - 1):
        coarse_relax(coarse[2], at)
        at = 1 - at
    for C, D in ((coarse[1], coarse[2]), (coarse[0], coarse[1])):
        coarse_up(C, D, 1, at)
        coarse_relax(C, 1)
        coarse_relax(C, 0)
        at = 1

    packed = jnp.zeros(tile, jnp.float32)
    for x in range(XC):
        for c in range(2):
            value = va[1, c, ix * XC + x + 1]
            only = jnp.where(clane % 4 == iz, value, 0.0)
            back = only + roll(only, 1, 1)
            back = back + roll(back, 2, 1)
            ahead = only + roll(only, LANES - 1, 1)
            ahead = ahead + roll(ahead, LANES - 2, 1)
            own[c, x] = jnp.where(clane % 4 <= iz, ahead, back)
    for x in range(XC):
        add = []
        for c in range(2):
            value = own[c, x, pl.ds(4 * iy, 1), :]
            full = jnp.broadcast_to(value, tile)
            for y in range(1, 4):
                value = own[c, x, pl.ds(4 * iy + y, 1), :]
                full = jnp.where(row >= 4 * y, value, full)
            add.append(full)
        for half_ in range(2):
            values = [v1[1, c, 2 * x + half_ + 1] + add[c] for c in range(2)]
            packed = put(half, 2, 2 * x + half_, values, packed)
    seal(half, 2, packed)
    bulk(gg, 1).wait_send()
    relax(half, 2)

    def store_half(x, values):
        for c in range(2):
            gl1[c, x] = values[c]

    last(half, 3, store_half)

    def up_plane(x, packed):
        values = [v0[1, c, x + 1] + gl1[c, x // 2] for c in range(2)]
        return put(fine, 2, x, values, packed)

    seal(fine, 2, lax.fori_loop(0, X0, up_plane, jnp.zeros(tile, jnp.float32), unroll=True))
    relax(fine, 2)

    def store_out(x, values):
        for c in range(2):
            out[c, x] = values[c]

    last(fine, 3, store_out)

    for earlier in flying:
        sent(*earlier)


def solution(mesh):
    sizes = tuple(mesh.shape[a] for a in AXES)
    nx, ny, nz = sizes
    count = nx * ny * nz

    def shards(source, mach):
        _, X, Y, Z = source.shape
        assert X == 16 and Y == 16 and Z == LANES and nz == 4, "unsupported sizes"
        f32 = jnp.float32
        yall = ny * Y // 4
        xs = [nx * X // 2**l for l in (2, 3, 4)]
        scratch = [
            pltpu.VMEM(source.shape, f32),
            pltpu.VMEM(mach.shape, mach.dtype),
            pltpu.SemaphoreType.DMA((2,)),
            pltpu.VMEM((4, 2, X + 2, Y, LANES), f32),
            pltpu.VMEM((4, 2, X // 2 + 2, Y, LANES), f32),
            pltpu.VMEM((2, X // 2, Y, LANES), f32),
            pltpu.VMEM((4, X, Y, LANES), f32),
            pltpu.VMEM((4, X // 2, Y, LANES), f32),
            pltpu.VMEM((4, 2, 2, X, LANES), f32),
            pltpu.VMEM((4, 2, 2, X, LANES), f32),
            pltpu.VMEM((4, 2, 2, X // 2, LANES), f32),
            pltpu.VMEM((4, 2, 2, X // 2, LANES), f32),
            pltpu.VMEM((8, Y, LANES), f32),
            pltpu.VMEM((8, 2, Y, LANES), f32),
            pltpu.VMEM((count, 8, LANES), f32),
            pltpu.VMEM((count, 8, LANES), f32),
        ]
        scratch += [pltpu.VMEM((2, 2, n + 2, yall, LANES), f32) for n in xs]
        scratch += [pltpu.VMEM((2, n, yall, LANES), f32) for n in xs]
        scratch += [pltpu.VMEM((4, n, yall, LANES), f32) for n in xs]
        scratch += [
            pltpu.VMEM((2, X // 4, yall, LANES), f32),
            pltpu.SemaphoreType.DMA((8, 6)),
            pltpu.SemaphoreType.DMA((8, 6)),
            pltpu.SemaphoreType.DMA((2,)),
            pltpu.SemaphoreType.DMA((2,)),
        ]
        return pl.pallas_call(
            functools.partial(kernel, sizes),
            out_shape=jax.ShapeDtypeStruct(source.shape, f32),
            in_specs=[pl.BlockSpec(memory_space=pltpu.HBM)] * 2,
            out_specs=pl.BlockSpec(memory_space=pltpu.VMEM),
            scratch_shapes=scratch,
            compiler_params=pltpu.CompilerParams(
                collective_id=0, has_side_effects=True, vmem_limit_bytes=60 * 2**20
            ),
        )(source, mach)

    return jax.shard_map(
        shards,
        mesh=mesh,
        in_specs=(P(None, "gx", "gy", "gz"), P("gx", "gy", "gz")),
        out_specs=P(None, "gx", "gy", "gz"),
        check_vma=False,
    )
```
